128 devices in a mesh: row: 8 (over z_lo, y), col: 16 (over z_hi, x, core).
Axes of the slice: x: 4, y: 4, z: 4 (z_hi: 2, z_lo: 2; z = z_hi * 2 + z_lo), core: 2. Of those that a mesh axis runs over, the one named last changes fastest.
Arguments:
- picture_vectors: float32 [8192, 1152], P(('row', 'col')), may hold values from -4 to 4
- caption_vectors: float32 [32768, 1152], P(('row', 'col')), may hold values from -4 to 4
- matching_captions: int32 [8192], replicated, may hold values from 0 to 32767, as said below
- natural_exponent_coefficient: float32 [1], replicated, may hold values from 2.3 to 3
- learned_shift: float32 [1], replicated, may hold values from -8 to -6
Outputs:
- grad_images: float32 [8192, 1152], P(('row', 'col'))
- grad_texts: float32 [32768, 1152], P(('row', 'col'))
- loss: float32 [], replicated
The draws below stay inside these ranges and needn't reach their ends.
Inputs may be any that keep to these rules, and one draw needn't show every extreme that they name: `matching_captions`: no two images name the same text; every value is a text row below 32768.
All inputs are finite; a program needn't handle non-finite values.
Results may differ from the reference program's by a relative error of at most 0.0016.
The reference program's roundings to bfloat16 on the way count: a program that leaves them out, or rounds other values in their place, can miss the bound.
Values may be sent and summed in bfloat16 or wider, within the bound.
No kernel may reach another device: no remote copies, remote signals or barrier semaphores. Data moves between devices by JAX's collectives and lax.ppermute only.
A program may use at most 128 MiB of HBM per device.

```python
import math
import jax
import jax.numpy as jnp
from jax import lax

D = 1152
NI = 8192
NT = 32768
N_ROW = 8
N_COL = 16


def layout(key):
    keys = jax.random.split(jax.random.fold_in(key, 11), 6)
    middle = jax.random.permutation(keys[0], NT - 2)[:NI - 2].astype(jnp.int32) + 1
    values = jnp.concatenate([jnp.zeros((1,), jnp.int32), jnp.full((1,), NT - 1, jnp.int32), middle])
    order = jax.random.permutation(keys[1], NI)
    matching_captions = values[order].astype(jnp.int32)
    groups = max(NI // 16, 2)
    image_group = jax.random.randint(keys[2], (NI,), 0, groups).astype(jnp.int32)
    text_group = jax.random.randint(keys[3], (NT,), 0, groups).astype(jnp.int32)
    text_group = text_group.at[matching_captions].set(image_group)
    centers = jax.random.truncated_normal(keys[4], -4.0, 4.0, (groups, D), jnp.float32)
    image_noise = jax.random.truncated_normal(keys[5], -4.0, 4.0, (NI, D), jnp.float32)
    return (matching_captions, image_group, text_group, centers, image_noise)


def row_scales(key, count, top):
    return jnp.exp(jax.random.uniform(key, (count, 1), jnp.float32, math.log(0.1), math.log(top)))


def draw_matching_captions(key, part):
    matching_captions, image_group, text_group, centers, image_noise = layout(key)
    return matching_captions.astype(jnp.int32)


def draw_picture_vectors(key, part):
    matching_captions, image_group, text_group, centers, image_noise = layout(key)
    key = jax.random.fold_in(key, 3)
    strength, top = (0.8, 1.0)
    raw = strength * centers[image_group] + image_noise
    scaled = row_scales(key, NI, top) * raw
    return jnp.clip(scaled, -4.0, 4.0).astype(jnp.float32)


def draw_caption_vectors(key, part):
    matching_captions, image_group, text_group, centers, image_noise = layout(key)
    key = jax.random.fold_in(key, 5)
    noise_key, scale_key = jax.random.split(key)
    strength, carried, top = (0.8, 0.8, 1.0)
    own_noise = jax.random.truncated_normal(noise_key, -4.0, 4.0, (NT, D), jnp.float32)
    matched = jnp.zeros((NT, D), jnp.float32).at[matching_captions].set(image_noise)
    raw = strength * centers[text_group] + own_noise + carried * matched
    scaled = row_scales(scale_key, NT, top) * raw
    return jnp.clip(scaled, -4.0, 4.0).astype(jnp.float32)


def setup_inputs(seed: int = 0) -> dict:
    seeds = jax.random.split(jax.random.key(seed), 6)
    picture_vectors = draw_picture_vectors(jax.random.fold_in(seeds[5], 71), 0)
    caption_vectors = draw_caption_vectors(jax.random.fold_in(seeds[5], 71), 0)
    matching_captions = draw_matching_captions(jax.random.fold_in(seeds[5], 71), 0)
    natural_exponent_coefficient = jnp.clip(jax.random.uniform(seeds[3], (1,), jnp.float32, 2.3, 3.0), 2.3, 3.0)
    learned_shift = jnp.clip(jax.random.uniform(seeds[4], (1,), jnp.float32, -8.0, -6.0), -8.0, -6.0)
    return dict(picture_vectors=picture_vectors, caption_vectors=caption_vectors, matching_captions=matching_captions, natural_exponent_coefficient=natural_exponent_coefficient, learned_shift=learned_shift)


def unit_rows(matrix):
    inverse = 1.0 / jnp.sqrt(lax.optimization_barrier(jnp.sum(matrix * matrix, axis=1, keepdims=True)) + 1e-06)
    return (matrix * inverse, inverse)

def finish(unit_vals, inverse, direction):
    return inverse * (direction - unit_vals * lax.optimization_barrier(jnp.sum(unit_vals * direction, axis=1, keepdims=True)))

def reference(picture_vectors, caption_vectors, matching_captions, natural_exponent_coefficient, learned_shift):
    image_unit, image_inv = unit_rows(picture_vectors)
    text_unit, text_inv = unit_rows(caption_vectors)
    image_bf = image_unit.astype(jnp.bfloat16)
    caption_reduced_float = text_unit.astype(jnp.bfloat16)
    sharpness_factor = jnp.exp(natural_exponent_coefficient[0])
    score_shift = learned_shift[0]
    blocks = N_ROW * N_COL
    height = NI // blocks
    caption_index_start = jnp.arange(NT, dtype=jnp.int32)

    def step_block(carry, pieces):
        loss_sum, text_acc = carry
        panel_reduced_float, block_pos = pieces
        couple_scores = sharpness_factor * jnp.dot(panel_reduced_float, caption_reduced_float.T, preferred_element_type=jnp.float32) + score_shift
        couple_labels_sign = jnp.where(block_pos[:, None] == caption_index_start[None, :], 1.0, -1.0).astype(jnp.float32)
        oriented_scores = couple_labels_sign * couple_scores
        loss_sum = loss_sum + jnp.sum(jax.nn.softplus(-oriented_scores))
        couple_factor = (-couple_labels_sign * jax.nn.sigmoid(-oriented_scores) * sharpness_factor).astype(jnp.bfloat16)
        image_dir = jnp.dot(couple_factor, caption_reduced_float, preferred_element_type=jnp.float32)
        text_acc = text_acc + jnp.dot(couple_factor.T, panel_reduced_float, preferred_element_type=jnp.float32)
        return ((loss_sum, text_acc), image_dir)
    start_carry = (jnp.zeros((), jnp.float32), jnp.zeros((NT, D), jnp.float32))
    pieces = (image_bf.reshape(blocks, height, D), matching_captions.reshape(blocks, height))
    (loss_sum, text_dir), image_dirs = lax.scan(step_block, start_carry, pieces)
    image_dir = image_dirs.reshape(NI, D)
    grad_images = finish(image_unit, image_inv, image_dir)
    grad_texts = finish(text_unit, text_inv, text_dir)
    return (grad_images, grad_texts, loss_sum / NI)
```

```python
import functools
import math

import jax
import jax.numpy as jnp
from jax import lax
from jax.experimental import pallas as pl
from jax.experimental.pallas import tpu as pltpu
from jax.sharding import PartitionSpec as P

AXES = ("row", "col")
RING = 4
LOG2E = math.log2(math.e)
WIRE = jnp.float16


def place(index):
    row, col = index // 16, index % 16
    return (col // 2) % 4, row % 4, (col // 8) * 2 + row // 4, col % 2


def index_of(x, y, z, core):
    return ((z % 2) * 4 + y) * 16 + (z // 2) * 8 + x * 2 + core


def send(value, move):
    pairs = [(d, index_of(*move(*place(d)))) for d in range(128)]
    return lax.ppermute(value, AXES, pairs)


def along_y(step):
    return lambda x, y, z, c: (x, (y + step) % RING, z, c)


def along_first(step):
    return lambda x, y, z, c: ((x + step) % RING, y, z, c) if c == 0 else (x, y, (z + step) % RING, c)


def along_second(step):
    return lambda x, y, z, c: (x, y, (z + step) % RING, c) if c == 0 else ((x + step) % RING, y, z, c)


def swap(x, y, z, c):
    return x, y, z, 1 - c


def unit_rows(matrix):
    inverse = 1.0 / jnp.sqrt(jnp.sum(matrix * matrix, axis=1, keepdims=True) + 1e-06)
    return (matrix * inverse, inverse)


def finish(unit_vals, inverse, direction):
    return inverse * (direction - unit_vals * jnp.sum(unit_vals * direction, axis=1, keepdims=True))


CHUNK = 256


def pair_kernel(scale_ref, base_ref, match_ref, *refs):
    texts, images = refs[:8], refs[8:12]
    image_out, text_out, loss_out = refs[12:15]
    text_buf, image_buf, weight_buf, sems = refs[15:]
    copies = [
        pltpu.make_async_copy(src, image_buf.at[pl.ds(i * CHUNK, CHUNK)], sems.at[i])
        for i, src in enumerate(images)
    ] + [
        pltpu.make_async_copy(src, text_buf.at[pl.ds(i * CHUNK, CHUNK)], sems.at[4 + i])
        for i, src in enumerate(texts)
    ]
    for copy in copies:
        copy.start()
    slope, shift, temperature = scale_ref[0], scale_ref[1], scale_ref[2]
    image_out[...] = jnp.zeros_like(image_out)
    loss_out[...] = jnp.zeros_like(loss_out)
    for copy in copies:
        copy.wait()
    row_index = lax.broadcasted_iota(jnp.int32, (CHUNK, CHUNK), 0)

    def step(s, carry):
        for half in range(2):
            rows = pl.ds(s * 2 * CHUNK + half * CHUNK, CHUNK)
            base = base_ref[2 * s + half]
            for i in range(4):
                cols = pl.ds(i * CHUNK, CHUNK)
                scores = lax.dot_general(
                    text_buf[rows, :],
                    image_buf[cols, :],
                    (((1,), (1,)), ((), ())),
                    preferred_element_type=jnp.float32,
                )
                matched = (match_ref[:, cols] - base) == row_index
                power = scores * slope + shift
                grown = jnp.exp2(jnp.where(matched, -power, power))
                total = 1.0 + grown
                inv = pl.reciprocal(total, approx=True)
                inv = inv * (2.0 - total * inv)
                weight = (grown * temperature) * inv
                weight = jnp.where(matched, -weight, weight)
                weight_buf[pl.ds(half * CHUNK, CHUNK), cols] = weight.astype(jnp.bfloat16)
                low, high = grown[: CHUNK // 2], grown[CHUNK // 2 :]
                joined = low + high + low * high
                low, high = joined[: CHUNK // 4], joined[CHUNK // 4 :]
                joined = low + high + low * high
                loss_out[...] += jnp.sum(jnp.log1p(joined).reshape(8, 8, CHUNK), axis=0)
        rows = pl.ds(s * 2 * CHUNK, 2 * CHUNK)
        text_out[rows, :] = jnp.dot(
            weight_buf[...], image_buf[...], preferred_element_type=jnp.float32
        )
        for i in range(4):
            cols = pl.ds(i * CHUNK, CHUNK)
            image_out[cols, :] += lax.dot_general(
                weight_buf[:, cols],
                text_buf[rows, :],
                (((0,), (0,)), ((), ())),
                preferred_element_type=jnp.float32,
            )
        return carry

    lax.fori_loop(0, 4, step, 0)


def pair_block(scale, base, match, texts, images):
    dim = images[0].shape[1]
    any_space = pl.BlockSpec(memory_space=pl.ANY)
    smem = pl.BlockSpec(memory_space=pltpu.SMEM)
    vmem = pl.BlockSpec(memory_space=pltpu.VMEM)
    return pl.pallas_call(
        pair_kernel,
        out_shape=(
            jax.ShapeDtypeStruct((4 * CHUNK, dim), jnp.float32),
            jax.ShapeDtypeStruct((8 * CHUNK, dim), jnp.float32),
            jax.ShapeDtypeStruct((8, CHUNK), jnp.float32),
        ),
        in_specs=[smem, smem, vmem] + [any_space] * 12,
        out_specs=(vmem, vmem, vmem),
        scratch_shapes=[
            pltpu.VMEM((8 * CHUNK, dim), jnp.bfloat16),
            pltpu.VMEM((4 * CHUNK, dim), jnp.bfloat16),
            pltpu.VMEM((2 * CHUNK, 4 * CHUNK), jnp.bfloat16),
            pltpu.SemaphoreType.DMA((12,)),
        ],
        compiler_params=pltpu.CompilerParams(vmem_limit_bytes=48 * 2**20),
        cost_estimate=pl.CostEstimate(
            flops=6 * 4 * CHUNK * 8 * CHUNK * dim,
            bytes_accessed=24 * 2**20,
            transcendentals=3 * 32 * CHUNK * CHUNK,
        ),
    )(scale, base, match, *texts, *images)


def body(
    picture_vectors, caption_vectors, matching_captions, natural_exponent_coefficient, learned_shift
):
    me = lax.axis_index("row") * 16 + lax.axis_index("col")
    x, y, z, core = place(me)
    image_rows, text_rows = picture_vectors.shape[0], caption_vectors.shape[0]
    temperature = jnp.exp(natural_exponent_coefficient[0])
    scale = jnp.stack([temperature * LOG2E, learned_shift[0] * LOG2E, temperature])

    text_unit, text_inv = unit_rows(caption_vectors)
    text_bf = text_unit.astype(jnp.bfloat16)
    image_unit, image_inv = unit_rows(picture_vectors)
    image_bf = image_unit.astype(jnp.bfloat16)

    own_texts = [text_bf] + [send(text_bf, along_y(-s)) for s in (1, 2, 3)]
    lines = [image_bf] + [send(image_bf, along_first(-r)) for r in (1, 2, 3)]
    line = jnp.concatenate(lines, axis=0)
    images = [line] + [send(line, along_second(-s)) for s in (1, 2, 3)]
    sibling_texts = [send(t, swap) for t in own_texts]
    texts = [t for pair in zip(own_texts, sibling_texts) for t in pair]

    base = jnp.stack(
        [index_of(x, (y + s) % RING, z, k) for s in range(RING) for k in (core, 1 - core)]
    ).astype(jnp.int32) * text_rows
    table = matching_captions.reshape(-1, image_rows)
    steps = jnp.arange(RING, dtype=jnp.int32)
    second, first = steps[:, None], steps[None, :]
    owners = jnp.where(
        core == 0,
        index_of((x + first) % RING, y, (z + second) % RING, core),
        index_of((x + second) % RING, y, (z + first) % RING, core),
    )
    match = jnp.take(table, owners.reshape(-1), axis=0).reshape(1, -1)

    image_part, text_part, loss_part = pair_block(scale, base, match, texts, images)

    text_part = text_part.reshape(RING, 2, text_rows, -1)
    other = text_part[:, 1].astype(WIRE)
    mine = text_part[:, 0] + send(other, swap).astype(jnp.float32)
    text_dir = mine[0]
    arrived = [send(mine[s].astype(WIRE), along_y(s)) for s in (1, 2, 3)]
    for part in arrived:
        text_dir = text_dir + part.astype(jnp.float32)

    image_part = image_part.reshape(RING, RING * image_rows, -1)
    arrived = [send(image_part[s].astype(WIRE), along_second(s)) for s in (1, 2, 3)]
    line_dir = image_part[0]
    for part in arrived:
        line_dir = line_dir + part.astype(jnp.float32)
    line_dir = line_dir.reshape(RING, image_rows, -1)
    arrived = [send(line_dir[r].astype(WIRE), along_first(r)) for r in (1, 2, 3)]
    image_dir = line_dir[0]
    for part in arrived:
        image_dir = image_dir + part.astype(jnp.float32)

    grad_images = finish(image_unit, image_inv, image_dir)
    grad_texts = finish(text_unit, text_inv, text_dir)
    loss = lax.psum(jnp.sum(loss_part), AXES) / matching_captions.shape[0]
    return (grad_images, grad_texts, loss)


def solution(mesh):
    placed = (P(AXES, None), P(AXES, None), P(), P(), P())
    return jax.shard_map(
        body,
        mesh=mesh,
        in_specs=placed,
        out_specs=(P(AXES, None), P(AXES, None), P()),
        check_vma=False,
    )
```

```python
import functools
import math

import jax
import jax.numpy as jnp
from jax import lax
from jax.experimental import pallas as pl
from jax.experimental.pallas import tpu as pltpu
from jax.sharding import PartitionSpec as P

AXES = ("row", "col")
RING = 4
LOG2E = math.log2(math.e)
WIRE = jnp.float16


def place(index):
    row, col = index // 16, index % 16
    return (col // 2) % 4, row % 4, (col // 8) * 2 + row // 4, col % 2


def index_of(x, y, z, core):
    return ((z % 2) * 4 + y) * 16 + (z // 2) * 8 + x * 2 + core


def send(value, move):
    pairs = [(d, index_of(*move(*place(d)))) for d in range(128)]
    return lax.ppermute(value, AXES, pairs)


def along_y(step):
    return lambda x, y, z, c: (x, (y + step) % RING, z, c)


def along_first(step):
    return lambda x, y, z, c: ((x + step) % RING, y, z, c) if c == 0 else (x, y, (z + step) % RING, c)


def along_second(step):
    return lambda x, y, z, c: (x, y, (z + step) % RING, c) if c == 0 else ((x + step) % RING, y, z, c)


def swap(x, y, z, c):
    return x, y, z, 1 - c


def finish(unit_vals, inverse, direction):
    return inverse * (direction - unit_vals * jnp.sum(unit_vals * direction, axis=1, keepdims=True))


CHUNK = 256
BLOCK = 512
VMEM = pl.BlockSpec(memory_space=pltpu.VMEM)
SMEM = pl.BlockSpec(memory_space=pltpu.SMEM)
ANY = pl.BlockSpec(memory_space=pl.ANY)
HBM = pl.BlockSpec(memory_space=pltpu.HBM)


def prepare_kernel(text_ref, image_ref, text_bf, text_inv, image_bf, image_inv):
    for src, unit, inv in ((image_ref, image_bf, image_inv), (text_ref, text_bf, text_inv)):
        matrix = src[...]
        inverse = 1.0 / jnp.sqrt(jnp.sum(matrix * matrix, axis=1, keepdims=True) + 1e-06)
        inv[...] = inverse
        rows = (matrix * inverse).astype(jnp.bfloat16)
        if unit.ndim == 2:
            unit[...] = rows
        else:
            for i in range(unit.shape[0]):
                unit[i] = rows


def prepare(texts, images):
    return pl.pallas_call(
        prepare_kernel,
        out_shape=(
            jax.ShapeDtypeStruct((RING,) + texts.shape, jnp.bfloat16),
            jax.ShapeDtypeStruct((texts.shape[0], 1), jnp.float32),
            jax.ShapeDtypeStruct(images.shape, jnp.bfloat16),
            jax.ShapeDtypeStruct((images.shape[0], 1), jnp.float32),
        ),
        in_specs=[VMEM] * 2,
        out_specs=[VMEM] * 4,
    )(texts, images)


def nothing(*refs):
    pass


def held(value, others):
    return pl.pallas_call(
        nothing,
        out_shape=jax.ShapeDtypeStruct(value.shape, value.dtype),
        in_specs=[ANY] * (1 + len(others)),
        out_specs=ANY,
        input_output_aliases={0: 0},
    )(value, *others)


def after(value, others):
    for other in others:
        value = value + 0 * other[:1, : value.shape[1]].astype(value.dtype)
    return value


def pair_kernel(n_image, *refs):
    scale_ref, base_ref, pick_ref, match_ref = refs[:4]
    halves, images, refs = refs[4:6], refs[6 : 6 + n_image], refs[6 + n_image :]
    text_outs, image_outs = refs[:2], refs[2 : 2 + n_image]
    loss_out, text_buf, image_buf, weight_buf, sems = refs[2 + n_image :]
    n_cols, n_text = n_image, 2 * RING

    def tile(i):
        return pl.ds(pl.multiple_of(i * CHUNK, CHUNK), CHUNK)

    image_copies = [
        pltpu.make_async_copy(piece, image_buf.at[tile(i)], sems.at[n_text + i])
        for i, piece in enumerate(images)
    ]
    text_copies = [
        pltpu.make_async_copy(
            halves[t // RING].at[tile(pick_ref[t % RING])], text_buf.at[tile(t)], sems.at[t]
        )
        for t in range(n_text)
    ]
    for copy in text_copies[:1] + image_copies + text_copies[1:]:
        copy.start()
    slope, shift, temperature = scale_ref[0], scale_ref[1], scale_ref[2]
    loss_out[...] = jnp.zeros_like(loss_out)
    row_index = lax.broadcasted_iota(jnp.int32, (CHUNK, CHUNK), 0)

    for copy in image_copies:
        copy.wait()

    def weigh(t, carry):
        base = base_ref[t]
        pltpu.make_async_copy(text_buf.at[tile(t)], text_buf.at[tile(t)], sems.at[t]).wait()
        for i in range(n_cols):
            cols = pl.ds(i * CHUNK, CHUNK)
            scores = lax.dot_general(
                text_buf[tile(t), :],
                image_buf[cols, :],
                (((1,), (1,)), ((), ())),
                preferred_element_type=jnp.float32,
            )
            matched = (match_ref[:, cols] - base) == row_index
            power = scores * slope + shift
            grown = jnp.exp2(jnp.where(matched, -power, power))
            total = 1.0 + grown
            inv = pl.reciprocal(total, approx=True)
            inv = inv * (2.0 - total * inv)
            weight = (grown * temperature) * inv
            weight = jnp.where(matched, -weight, weight)
            weight_buf[tile(t), cols] = weight.astype(jnp.bfloat16)
            low, high = grown[: CHUNK // 2], grown[CHUNK // 2 :]
            joined = low + high + low * high
            low, high = joined[: CHUNK // 4], joined[CHUNK // 4 :]
            joined = low + high + low * high
            loss_out[...] += jnp.sum(jnp.log1p(joined).reshape(8, 8, CHUNK), axis=0)
        return carry

    lax.fori_loop(0, n_text, weigh, 0)

    for half, out in enumerate(text_outs):
        rows = pl.ds(half * RING * CHUNK, RING * CHUNK)
        out[...] = jnp.dot(
            weight_buf[rows, :], image_buf[...], preferred_element_type=jnp.float32
        )

    for i, out in enumerate(image_outs):
        out[...] = lax.dot_general(
            weight_buf[:, pl.ds(i * CHUNK, CHUNK)],
            text_buf[...],
            (((0,), (0,)), ((), ())),
            preferred_element_type=jnp.float32,
        )


def slow(*arrays):
    return [pltpu.with_memory_space_constraint(a, pltpu.HBM) for a in arrays]


def pair_block(scale, base, pick, match, mine, other, images):
    n_image, dim = len(images), mine.shape[1]
    n_rows, n_cols = 2 * RING * CHUNK, n_image * CHUNK
    out_shape = [jax.ShapeDtypeStruct((n_rows // 2, dim), jnp.float32)] * 2
    out_shape += [jax.ShapeDtypeStruct((CHUNK, dim), jnp.float32)] * n_image
    out_shape += [jax.ShapeDtypeStruct((8, CHUNK), jnp.float32)]
    out = pl.pallas_call(
        functools.partial(pair_kernel, n_image),
        out_shape=out_shape,
        in_specs=[SMEM, SMEM, SMEM, VMEM] + [HBM] * (2 + n_image),
        out_specs=[VMEM] * len(out_shape),
        scratch_shapes=[
            pltpu.VMEM((n_rows, dim), jnp.bfloat16),
            pltpu.VMEM((n_cols, dim), jnp.bfloat16),
            pltpu.VMEM((n_rows, n_cols), jnp.bfloat16),
            pltpu.SemaphoreType.DMA((2 * RING + n_image,)),
        ],
        compiler_params=pltpu.CompilerParams(vmem_limit_bytes=VMEM_LIMIT),
        cost_estimate=pl.CostEstimate(
            flops=6 * n_rows * n_cols * dim,
            bytes_accessed=2 * (n_rows + n_cols) * dim,
            transcendentals=2 * n_rows * n_cols,
        ),
    )(scale, base, pick, match, *slow(mine, other, *images))
    return out[0], out[1], out[2:-1], out[-1]


VMEM_LIMIT = 32 * 2**20


def total_loss(part):
    part = jnp.sum(part.reshape(-1, 128), axis=0)[None, None]
    parts = jnp.broadcast_to(part, (128, 1, 128))
    return jnp.sum(lax.all_to_all(parts, AXES, 0, 0, tiled=True))


def narrow(part):
    return (part * 0.25).astype(WIRE)


def wide(part):
    return part.astype(jnp.float32) * 4.0


def body(
    picture_vectors, caption_vectors, matching_captions, natural_exponent_coefficient, learned_shift
):
    me = lax.axis_index("row") * 16 + lax.axis_index("col")
    x, y, z, core = place(me)
    image_rows, text_rows = picture_vectors.shape[0], caption_vectors.shape[0]
    temperature = jnp.exp(natural_exponent_coefficient[0])
    scale = jnp.stack([temperature * LOG2E, learned_shift[0] * LOG2E, temperature])

    own, text_inv, image_bf, image_inv = prepare(caption_vectors, picture_vectors)

    rings = {}
    for d in range(128):
        at = place(d)
        rings.setdefault(at[:1] + at[2:], []).append(d)
    mine = lax.all_to_all(own, AXES, 0, 0, axis_index_groups=list(rings.values()), tiled=True)
    mine = mine.reshape(RING * text_rows, -1)
    line = jnp.concatenate([image_bf] + [send(image_bf, along_first(-r)) for r in (1, 2, 3)])
    image_up, image_down = send(line, along_second(-1)), send(line, along_second(1))
    image_far = send(line, along_second(2))
    images = [line, image_up, image_down, image_far]
    mine = held(mine, images)
    other = send(mine, swap)

    pick = (jnp.arange(RING, dtype=jnp.int32) + y) % RING
    mine_base = index_of(x, pick, z, core) * text_rows
    other_base = index_of(x, pick, z, 1 - core) * text_rows
    table = matching_captions.reshape(-1, image_rows)
    first = jnp.arange(RING, dtype=jnp.int32)[None, :]
    second = jnp.array([0, 1, 3, 2], dtype=jnp.int32)[:, None]
    owners = jnp.where(
        core == 0,
        index_of((x + first) % RING, y, (z + second) % RING, core),
        index_of((x + second) % RING, y, (z + first) % RING, core),
    )
    match = jnp.take(table, owners.reshape(-1), axis=0).reshape(1, -1)

    n = text_rows
    base = jnp.concatenate([mine_base, other_base])
    mine, other, parts, loss = pair_block(scale, base, pick, match, mine, other, images)
    n = text_rows
    other = send(narrow(other), swap)
    wires = [
        narrow(mine[s * n : (s + 1) * n] + wide(other[s * n : (s + 1) * n])) for s in (1, 3, 2)
    ]
    text_dir = mine[:n] + wide(other[:n])
    for s, wire in zip((1, 3, 2), wires):
        text_dir = text_dir + wide(send(wire, along_y(s)))

    line_dir, up_part, down_part, far_part = parts
    far_part = held(far_part, [wide(wires[0][:8, :128])])
    for s, part in ((1, up_part), (3, down_part), (2, far_part)):
        line_dir = line_dir + wide(send(narrow(part), along_second(s)))
    loss = total_loss(after(loss, [line_dir]))
    n = image_rows
    wire = narrow(line_dir[n:])
    image_dir = line_dir[:n]
    for r in (1, 2, 3):
        image_dir = image_dir + wide(send(wire[(r - 1) * n : r * n], along_first(r)))

    grad_images = finish(picture_vectors * image_inv, image_inv, image_dir)
    grad_texts = finish(caption_vectors * text_inv, text_inv, text_dir)
    loss = loss / matching_captions.shape[0]
    return (grad_images, grad_texts, loss)


def solution(mesh):
    placed = (P(AXES, None), P(AXES, None), P(), P(), P())
    return jax.shard_map(
        body,
        mesh=mesh,
        in_specs=placed,
        out_specs=(P(AXES, None), P(AXES, None), P()),
        check_vma=False,
    )
```

```python
import functools
import math

import jax
import jax.numpy as jnp
from jax import lax
from jax.experimental import pallas as pl
from jax.experimental.pallas import tpu as pltpu
from jax.sharding import PartitionSpec as P

AXES = ("row", "col")
RING = 4
LOG2E = math.log2(math.e)
WIRE = jnp.float16


def place(index):
    row, col = index // 16, index % 16
    return (col // 2) % 4, row % 4, (col // 8) * 2 + row // 4, col % 2


def index_of(x, y, z, core):
    return ((z % 2) * 4 + y) * 16 + (z // 2) * 8 + x * 2 + core


def send(value, move):
    pairs = [(d, index_of(*move(*place(d)))) for d in range(128)]
    return lax.ppermute(value, AXES, pairs)


def along_y(step):
    return lambda x, y, z, c: (x, (y + step) % RING, z, c)


def along_first(step):
    return lambda x, y, z, c: ((x + step) % RING, y, z, c) if c == 0 else (x, y, (z + step) % RING, c)


def along_second(step):
    return lambda x, y, z, c: (x, y, (z + step) % RING, c) if c == 0 else ((x + step) % RING, y, z, c)


def swap(x, y, z, c):
    return x, y, z, 1 - c


CHUNK = 256
BLOCK = 512
VMEM = pl.BlockSpec(memory_space=pltpu.VMEM)
SMEM = pl.BlockSpec(memory_space=pltpu.SMEM)
ANY = pl.BlockSpec(memory_space=pl.ANY)
HBM = pl.BlockSpec(memory_space=pltpu.HBM)


def prepare_kernel(text_ref, image_ref, text_bf, text_inv, image_bf, image_inv):
    for src, unit, inv in ((image_ref, image_bf, image_inv), (text_ref, text_bf, text_inv)):
        matrix = src[...]
        inverse = 1.0 / jnp.sqrt(jnp.sum(matrix * matrix, axis=1, keepdims=True) + 1e-06)
        inv[...] = inverse
        rows = (matrix * inverse).astype(jnp.bfloat16)
        if unit.ndim == 2:
            unit[...] = rows
        else:
            for i in range(unit.shape[0]):
                unit[i] = rows


def prepare(texts, images):
    return pl.pallas_call(
        prepare_kernel,
        out_shape=(
            jax.ShapeDtypeStruct((RING,) + texts.shape, jnp.bfloat16),
            jax.ShapeDtypeStruct((texts.shape[0], 1), jnp.float32),
            jax.ShapeDtypeStruct(images.shape, jnp.bfloat16),
            jax.ShapeDtypeStruct((images.shape[0], 1), jnp.float32),
        ),
        in_specs=[VMEM] * 2,
        out_specs=[VMEM] * 4,
    )(texts, images)


def nothing(*refs):
    pass


def held(value, others):
    return pl.pallas_call(
        nothing,
        out_shape=jax.ShapeDtypeStruct(value.shape, value.dtype),
        in_specs=[ANY] * (1 + len(others)),
        out_specs=ANY,
        input_output_aliases={0: 0},
    )(value, *others)


def after(value, others):
    for other in others:
        value = value + 0 * other[:1, :1].astype(value.dtype)
    return value


def finish_kernel(*refs):
    loss_parts, (image_out, text_out, loss_out) = refs[6], refs[7:]
    for (vectors, inverse, direction), out in ((refs[:3], image_out), (refs[3:6], text_out)):
        unit = vectors[...] * inverse[...]
        along = jnp.sum(unit * direction[...], axis=1, keepdims=True)
        out[...] = inverse[...] * (direction[...] - unit * along)
    total = jnp.sum(jnp.sum(loss_parts[...], axis=0), axis=1, keepdims=True)
    loss_out[...] = total * (1.0 / (128 * image_out.shape[0]))


def finish(images, texts, loss_parts):
    return pl.pallas_call(
        finish_kernel,
        out_shape=(
            jax.ShapeDtypeStruct(images[2].shape, jnp.float32),
            jax.ShapeDtypeStruct(texts[2].shape, jnp.float32),
            jax.ShapeDtypeStruct((1, 1), jnp.float32),
        ),
        in_specs=[VMEM] * 7,
        out_specs=[VMEM] * 3,
    )(*images, *texts, loss_parts)


def pair_kernel(n_image, *refs):
    scale_ref, base_ref, pick_ref, match_ref = refs[:4]
    halves, images, refs = refs[4:6], refs[6 : 6 + n_image], refs[6 + n_image :]
    text_outs, image_outs = refs[:2], refs[2 : 2 + n_image]
    loss_out, text_buf, image_buf, weight_buf, sems = refs[2 + n_image :]
    n_cols, n_text = n_image, 2 * RING

    def tile(i):
        return pl.ds(pl.multiple_of(i * CHUNK, CHUNK), CHUNK)

    image_copies = [
        pltpu.make_async_copy(piece, image_buf.at[tile(i)], sems.at[n_text + i])
        for i, piece in enumerate(images)
    ]
    text_copies = [
        pltpu.make_async_copy(
            halves[t // RING].at[tile(pick_ref[t % RING])], text_buf.at[tile(t)], sems.at[t]
        )
        for t in range(n_text)
    ]
    for copy in text_copies[:1] + image_copies + text_copies[1:]:
        copy.start()
    slope, shift, temperature = scale_ref[0], scale_ref[1], scale_ref[2]
    loss_out[...] = jnp.zeros_like(loss_out)
    row_index = lax.broadcasted_iota(jnp.int32, (CHUNK, CHUNK), 0)

    def weigh(t, carry, arriving=()):
        base = base_ref[t]
        pltpu.make_async_copy(text_buf.at[tile(t)], text_buf.at[tile(t)], sems.at[t]).wait()
        for i in range(n_cols):
            cols = pl.ds(i * CHUNK, CHUNK)
            if arriving:
                arriving[i].wait()
            scores = lax.dot_general(
                text_buf[tile(t), :],
                image_buf[cols, :],
                (((1,), (1,)), ((), ())),
                preferred_element_type=jnp.float32,
            )
            matched = (match_ref[:, cols] - base) == row_index
            power = scores * slope + shift
            grown = jnp.exp2(jnp.where(matched, -power, power))
            total = 1.0 + grown
            inv = pl.reciprocal(total, approx=True)
            inv = inv * (2.0 - total * inv)
            weight = (grown * temperature) * inv
            weight = jnp.where(matched, -weight, weight)
            weight_buf[tile(t), cols] = weight.astype(jnp.bfloat16)
            low, high = grown[: CHUNK // 2], grown[CHUNK // 2 :]
            joined = low + high + low * high
            low, high = joined[: CHUNK // 4], joined[CHUNK // 4 :]
            joined = low + high + low * high
            loss_out[...] += jnp.sum(jnp.log1p(joined).reshape(8, 8, CHUNK), axis=0)
        return carry

    weigh(0, 0, image_copies)
    lax.fori_loop(1, n_text, weigh, 0)

    for half, out in enumerate(text_outs):
        rows = pl.ds(half * RING * CHUNK, RING * CHUNK)
        out[...] = jnp.dot(
            weight_buf[rows, :], image_buf[...], preferred_element_type=jnp.float32
        )

    for i, out in enumerate(image_outs):
        out[...] = lax.dot_general(
            weight_buf[:, pl.ds(i * CHUNK, CHUNK)],
            text_buf[...],
            (((0,), (0,)), ((), ())),
            preferred_element_type=jnp.float32,
        )


def slow(*arrays):
    return [pltpu.with_memory_space_constraint(a, pltpu.HBM) for a in arrays]


def pair_block(scale, base, pick, match, mine, other, images):
    n_image, dim = len(images), mine.shape[1]
    n_rows, n_cols = 2 * RING * CHUNK, n_image * CHUNK
    out_shape = [jax.ShapeDtypeStruct((n_rows // 2, dim), jnp.float32)] * 2
    out_shape += [jax.ShapeDtypeStruct((CHUNK, dim), jnp.float32)] * n_image
    out_shape += [jax.ShapeDtypeStruct((8, CHUNK), jnp.float32)]
    out = pl.pallas_call(
        functools.partial(pair_kernel, n_image),
        out_shape=out_shape,
        in_specs=[SMEM, SMEM, SMEM, VMEM, HBM, ANY] + [HBM] * n_image,
        out_specs=[VMEM] * len(out_shape),
        scratch_shapes=[
            pltpu.VMEM((n_rows, dim), jnp.bfloat16),
            pltpu.VMEM((n_cols, dim), jnp.bfloat16),
            pltpu.VMEM((n_rows, n_cols), jnp.bfloat16),
            pltpu.SemaphoreType.DMA((2 * RING + n_image,)),
        ],
        compiler_params=pltpu.CompilerParams(vmem_limit_bytes=VMEM_LIMIT),
        cost_estimate=pl.CostEstimate(
            flops=6 * n_rows * n_cols * dim,
            bytes_accessed=2 * (n_rows + n_cols) * dim,
            transcendentals=2 * n_rows * n_cols,
        ),
    )(scale, base, pick, match, *slow(mine), other, *slow(*images))
    return out[0], out[1], out[2:-1], out[-1]


VMEM_LIMIT = 32 * 2**20


def loss_parts(part):
    part = jnp.sum(part.reshape(-1, 128), axis=0)[None, None]
    parts = jnp.broadcast_to(part, (128, 1, 128))
    return lax.all_to_all(parts, AXES, 0, 0, tiled=True)


def narrow(part):
    return (part * 0.25).astype(WIRE)


def wide(part):
    return part.astype(jnp.float32) * 4.0


def body(
    picture_vectors, caption_vectors, matching_captions, natural_exponent_coefficient, learned_shift
):
    me = lax.axis_index("row") * 16 + lax.axis_index("col")
    x, y, z, core = place(me)
    image_rows, text_rows = picture_vectors.shape[0], caption_vectors.shape[0]
    temperature = jnp.exp(natural_exponent_coefficient[0])
    scale = jnp.stack([temperature * LOG2E, learned_shift[0] * LOG2E, temperature])

    own, text_inv, image_bf, image_inv = prepare(caption_vectors, picture_vectors)

    rings = {}
    for d in range(128):
        at = place(d)
        rings.setdefault(at[:1] + at[2:], []).append(d)
    mine = lax.all_to_all(own, AXES, 0, 0, axis_index_groups=list(rings.values()), tiled=True)
    mine = mine.reshape(RING * text_rows, -1)
    line = jnp.concatenate([image_bf] + [send(image_bf, along_first(-r)) for r in (1, 2, 3)])
    image_up, image_down = send(line, along_second(-1)), send(line, along_second(1))
    image_far = send(line, along_second(2))
    images = [line, image_up, image_down, image_far]
    mine = held(mine, images)
    other = send(mine, swap)

    pick = (jnp.arange(RING, dtype=jnp.int32) + y) % RING
    mine_base = index_of(x, pick, z, core) * text_rows
    other_base = index_of(x, pick, z, 1 - core) * text_rows
    table = matching_captions.reshape(-1, image_rows)
    first = jnp.arange(RING, dtype=jnp.int32)[None, :]
    second = jnp.array([0, 1, 3, 2], dtype=jnp.int32)[:, None]
    owners = jnp.where(
        core == 0,
        index_of((x + first) % RING, y, (z + second) % RING, core),
        index_of((x + second) % RING, y, (z + first) % RING, core),
    )
    match = jnp.take(table, owners.reshape(-1), axis=0).reshape(1, -1)

    n = text_rows
    base = jnp.concatenate([mine_base, other_base])
    mine, other, parts, loss = pair_block(scale, base, pick, match, mine, other, images)
    n = text_rows
    other = send(narrow(other), swap)
    wires = [
        narrow(mine[s * n : (s + 1) * n] + wide(other[s * n : (s + 1) * n])) for s in (1, 3, 2)
    ]
    text_dir = mine[:n] + wide(other[:n])
    for s, wire in zip((1, 3, 2), wires):
        text_dir = text_dir + wide(send(wire, along_y(s)))

    line_dir, up_part, down_part, far_part = parts
    far_part = after(far_part, [wide(other[:8, :128])])
    for s, part in ((1, up_part), (3, down_part), (2, far_part)):
        line_dir = line_dir + wide(send(narrow(part), along_second(s)))
    loss = loss_parts(after(loss, [line_dir]))
    n = image_rows
    wire = narrow(line_dir[n:])
    image_dir = line_dir[:n]
    for r in (1, 2, 3):
        image_dir = image_dir + wide(send(wire[(r - 1) * n : r * n], along_first(r)))

    grad_images, grad_texts, loss = finish(
        (picture_vectors, image_inv, image_dir), (caption_vectors, text_inv, text_dir), loss
    )
    loss = loss[0, 0]
    return (grad_images, grad_texts, loss)


def solution(mesh):
    placed = (P(AXES, None), P(AXES, None), P(), P(), P())
    return jax.shard_map(
        body,
        mesh=mesh,
        in_specs=placed,
        out_specs=(P(AXES, None), P(AXES, None), P()),
        check_vma=False,
    )
```

```python
import functools
import math

import jax
import jax.numpy as jnp
from jax import lax
from jax.experimental import pallas as pl
from jax.experimental.pallas import tpu as pltpu
from jax.sharding import PartitionSpec as P

AXES = ("row", "col")
RING = 4
LOG2E = math.log2(math.e)
WIRE = jnp.float16


def place(index):
    row, col = index // 16, index % 16
    return (col // 2) % 4, row % 4, (col // 8) * 2 + row // 4, col % 2


def index_of(x, y, z, core):
    return ((z % 2) * 4 + y) * 16 + (z // 2) * 8 + x * 2 + core


def send(value, move):
    pairs = [(d, index_of(*move(*place(d)))) for d in range(128)]
    return lax.ppermute(value, AXES, pairs)


def along_y(step):
    return lambda x, y, z, c: (x, (y + step) % RING, z, c)


def along_first(step):
    return lambda x, y, z, c: ((x + step) % RING, y, z, c) if c == 0 else (x, y, (z + step) % RING, c)


def along_second(step):
    return lambda x, y, z, c: (x, y, (z + step) % RING, c) if c == 0 else ((x + step) % RING, y, z, c)


def swap(x, y, z, c):
    return x, y, z, 1 - c


CHUNK = 256
BLOCK = 512
VMEM = pl.BlockSpec(memory_space=pltpu.VMEM)
SMEM = pl.BlockSpec(memory_space=pltpu.SMEM)
ANY = pl.BlockSpec(memory_space=pl.ANY)
HBM = pl.BlockSpec(memory_space=pltpu.HBM)


def prepare_kernel(text_ref, image_ref, text_bf, text_inv, image_bf, image_inv):
    for src, unit, inv in ((image_ref, image_bf, image_inv), (text_ref, text_bf, text_inv)):
        matrix = src[...]
        inverse = 1.0 / jnp.sqrt(jnp.sum(matrix * matrix, axis=1, keepdims=True) + 1e-06)
        inv[...] = inverse
        rows = (matrix * inverse).astype(jnp.bfloat16)
        if unit.ndim == 2:
            unit[...] = rows
        else:
            for i in range(unit.shape[0]):
                unit[i] = rows


def prepare(texts, images):
    return pl.pallas_call(
        prepare_kernel,
        out_shape=(
            jax.ShapeDtypeStruct((RING,) + texts.shape, jnp.bfloat16),
            jax.ShapeDtypeStruct((texts.shape[0], 1), jnp.float32),
            jax.ShapeDtypeStruct(images.shape, jnp.bfloat16),
            jax.ShapeDtypeStruct((images.shape[0], 1), jnp.float32),
        ),
        in_specs=[VMEM] * 2,
        out_specs=[VMEM] * 4,
    )(texts, images)


def nothing(*refs):
    pass


def held(value, others):
    return pl.pallas_call(
        nothing,
        out_shape=jax.ShapeDtypeStruct(value.shape, value.dtype),
        in_specs=[ANY] * (1 + len(others)),
        out_specs=ANY,
        input_output_aliases={0: 0},
    )(value, *others)


def after(value, others):
    for other in others:
        value = value + 0 * other[:1, : value.shape[1]].astype(value.dtype)
    return value


def finish_kernel(*refs):
    loss_parts, (image_out, text_out, loss_out) = refs[6], refs[7:]
    for (vectors, inverse, direction), out in ((refs[:3], image_out), (refs[3:6], text_out)):
        unit = vectors[...] * inverse[...]
        along = jnp.sum(unit * direction[...], axis=1, keepdims=True)
        out[...] = inverse[...] * (direction[...] - unit * along)
    total = jnp.sum(jnp.sum(loss_parts[...], axis=0), axis=1, keepdims=True)
    loss_out[...] = total * (1.0 / (128 * image_out.shape[0]))


def finish(images, texts, loss_parts):
    return pl.pallas_call(
        finish_kernel,
        out_shape=(
            jax.ShapeDtypeStruct(images[2].shape, jnp.float32),
            jax.ShapeDtypeStruct(texts[2].shape, jnp.float32),
            jax.ShapeDtypeStruct((1, 1), jnp.float32),
        ),
        in_specs=[VMEM] * 7,
        out_specs=[VMEM] * 3,
    )(*images, *texts, loss_parts)


def pair_kernel(n_image, *refs):
    scale_ref, base_ref, pick_ref, match_ref = refs[:4]
    halves, images, refs = refs[4:6], refs[6 : 6 + n_image], refs[6 + n_image :]
    text_outs, image_outs = refs[:2], refs[2 : 2 + n_image]
    loss_out, text_buf, image_buf, weight_buf, sems = refs[2 + n_image :]
    n_cols, n_text = n_image, 2 * RING

    def tile(i):
        return pl.ds(pl.multiple_of(i * CHUNK, CHUNK), CHUNK)

    image_copies = [
        pltpu.make_async_copy(piece, image_buf.at[tile(i)], sems.at[n_text + i])
        for i, piece in enumerate(images)
    ]
    text_copies = [
        pltpu.make_async_copy(
            halves[t // RING].at[tile(pick_ref[t % RING])], text_buf.at[tile(t)], sems.at[t]
        )
        for t in range(n_text)
    ]
    for copy in text_copies[:1] + image_copies + text_copies[1:]:
        copy.start()
    slope, shift, temperature = scale_ref[0], scale_ref[1], scale_ref[2]
    loss_out[...] = jnp.zeros_like(loss_out)
    row_index = lax.broadcasted_iota(jnp.int32, (CHUNK, CHUNK), 0)

    def weigh(t, carry):
        base = base_ref[t]
        pltpu.make_async_copy(text_buf.at[tile(t)], text_buf.at[tile(t)], sems.at[t]).wait()
        for i in range(n_cols):
            cols = pl.ds(i * CHUNK, CHUNK)
            scores = lax.dot_general(
                text_buf[tile(t), :],
                image_buf[cols, :],
                (((1,), (1,)), ((), ())),
                preferred_element_type=jnp.float32,
            )
            matched = (match_ref[:, cols] - base) == row_index
            power = scores * slope + shift
            grown = jnp.exp2(jnp.where(matched, -power, power))
            total = 1.0 + grown
            inv = pl.reciprocal(total, approx=True)
            inv = inv * (2.0 - total * inv)
            weight = (grown * temperature) * inv
            weight = jnp.where(matched, -weight, weight)
            weight_buf[tile(t), cols] = weight.astype(jnp.bfloat16)
            low, high = grown[: CHUNK // 2], grown[CHUNK // 2 :]
            joined = low + high + low * high
            low, high = joined[: CHUNK // 4], joined[CHUNK // 4 :]
            joined = low + high + low * high
            loss_out[...] += jnp.sum(jnp.log1p(joined).reshape(8, 8, CHUNK), axis=0)
        return carry

    for copy in image_copies:
        copy.wait()
    lax.fori_loop(0, n_text, weigh, 0)

    for half, out in enumerate(text_outs):
        rows = pl.ds(half * RING * CHUNK, RING * CHUNK)
        out[...] = jnp.dot(
            weight_buf[rows, :], image_buf[...], preferred_element_type=jnp.float32
        )

    for i, out in enumerate(image_outs):
        out[...] = lax.dot_general(
            weight_buf[:, pl.ds(i * CHUNK, CHUNK)],
            text_buf[...],
            (((0,), (0,)), ((), ())),
            preferred_element_type=jnp.float32,
        )


def slow(*arrays):
    return [pltpu.with_memory_space_constraint(a, pltpu.HBM) for a in arrays]


def pair_block(scale, base, pick, match, mine, other, images):
    n_image, dim = len(images), mine.shape[1]
    n_rows, n_cols = 2 * RING * CHUNK, n_image * CHUNK
    out_shape = [jax.ShapeDtypeStruct((n_rows // 2, dim), jnp.float32)] * 2
    out_shape += [jax.ShapeDtypeStruct((CHUNK, dim), jnp.float32)] * n_image
    out_shape += [jax.ShapeDtypeStruct((8, CHUNK), jnp.float32)]
    out = pl.pallas_call(
        functools.partial(pair_kernel, n_image),
        out_shape=out_shape,
        in_specs=[SMEM, SMEM, SMEM, VMEM, HBM, ANY] + [HBM] * n_image,
        out_specs=[VMEM] * len(out_shape),
        scratch_shapes=[
            pltpu.VMEM((n_rows, dim), jnp.bfloat16),
            pltpu.VMEM((n_cols, dim), jnp.bfloat16),
            pltpu.VMEM((n_rows, n_cols), jnp.bfloat16),
            pltpu.SemaphoreType.DMA((2 * RING + n_image,)),
        ],
        compiler_params=pltpu.CompilerParams(vmem_limit_bytes=VMEM_LIMIT),
        cost_estimate=pl.CostEstimate(
            flops=6 * n_rows * n_cols * dim,
            bytes_accessed=2 * (n_rows + n_cols) * dim,
            transcendentals=2 * n_rows * n_cols,
        ),
    )(scale, base, pick, match, *slow(mine), other, *slow(*images))
    return out[0], out[1], out[2:-1], out[-1]


VMEM_LIMIT = 32 * 2**20


def loss_parts(part):
    part = jnp.sum(part.reshape(-1, 128), axis=0)[None, None]
    parts = jnp.broadcast_to(part, (128, 1, 128))
    return lax.all_to_all(parts, AXES, 0, 0, tiled=True)


def narrow(part):
    return (part * 0.25).astype(WIRE)


def wide(part):
    return part.astype(jnp.float32) * 4.0


def body(
    picture_vectors, caption_vectors, matching_captions, natural_exponent_coefficient, learned_shift
):
    me = lax.axis_index("row") * 16 + lax.axis_index("col")
    x, y, z, core = place(me)
    image_rows, text_rows = picture_vectors.shape[0], caption_vectors.shape[0]
    temperature = jnp.exp(natural_exponent_coefficient[0])
    scale = jnp.stack([temperature * LOG2E, learned_shift[0] * LOG2E, temperature])

    own, text_inv, image_bf, image_inv = prepare(caption_vectors, picture_vectors)

    rings = {}
    for d in range(128):
        at = place(d)
        rings.setdefault(at[:1] + at[2:], []).append(d)
    mine = lax.all_to_all(own, AXES, 0, 0, axis_index_groups=list(rings.values()), tiled=True)
    mine = mine.reshape(RING * text_rows, -1)
    line = jnp.concatenate([image_bf] + [send(image_bf, along_first(-r)) for r in (1, 2, 3)])
    image_up, image_down = send(line, along_second(-1)), send(line, along_second(1))
    image_far = send(line, along_second(2))
    images = [line, image_up, image_down, image_far]
    mine = held(mine, images)
    other = send(mine, swap)

    pick = (jnp.arange(RING, dtype=jnp.int32) + y) % RING
    mine_base = index_of(x, pick, z, core) * text_rows
    other_base = index_of(x, pick, z, 1 - core) * text_rows
    table = matching_captions.reshape(-1, image_rows)
    first = jnp.arange(RING, dtype=jnp.int32)[None, :]
    second = jnp.array([0, 1, 3, 2], dtype=jnp.int32)[:, None]
    owners = jnp.where(
        core == 0,
        index_of((x + first) % RING, y, (z + second) % RING, core),
        index_of((x + second) % RING, y, (z + first) % RING, core),
    )
    match = jnp.take(table, owners.reshape(-1), axis=0).reshape(1, -1)

    n = text_rows
    base = jnp.concatenate([mine_base, other_base])
    mine, other, parts, loss = pair_block(scale, base, pick, match, mine, other, images)
    n = text_rows
    other = send(narrow(other), swap)
    wires = [
        narrow(mine[s * n : (s + 1) * n] + wide(other[s * n : (s + 1) * n])) for s in (1, 3, 2)
    ]
    text_dir = lax.optimization_barrier(mine[:n] + wide(other[:n]))
    for s, wire in zip((1, 3, 2), wires):
        text_dir = text_dir + wide(send(wire, along_y(s)))

    line_dir, up_part, down_part, far_part = parts
    far_part = after(far_part, [other])
    for s, part in ((1, up_part), (3, down_part), (2, far_part)):
        line_dir = line_dir + wide(send(narrow(part), along_second(s)))
    loss = loss_parts(after(loss, [line_dir]))
    n = image_rows
    wire = narrow(line_dir[n:])
    image_dir = line_dir[:n]
    for r in (1, 2, 3):
        image_dir = image_dir + wide(send(wire[(r - 1) * n : r * n], along_first(r)))

    image_dir, text_dir = [
        pltpu.with_memory_space_constraint(a, pltpu.VMEM) for a in (image_dir, text_dir)
    ]
    grad_images, grad_texts, loss = finish(
        (picture_vectors, image_inv, image_dir), (caption_vectors, text_inv, text_dir), loss
    )
    loss = loss[0, 0]
    return (grad_images, grad_texts, loss)


def solution(mesh):
    placed = (P(AXES, None), P(AXES, None), P(), P(), P())
    return jax.shard_map(
        body,
        mesh=mesh,
        in_specs=placed,
        out_specs=(P(AXES, None), P(AXES, None), P()),
        check_vma=False,
    )
```

```python
import functools
import math

import jax
import jax.numpy as jnp
from jax import lax
from jax.experimental import pallas as pl
from jax.experimental.pallas import tpu as pltpu
from jax.sharding import PartitionSpec as P

AXES = ("row", "col")
RING = 4
LOG2E = math.log2(math.e)
WIRE = jnp.float16


def place(index):
    row, col = index // 16, index % 16
    return (col // 2) % 4, row % 4, (col // 8) * 2 + row // 4, col % 2


def index_of(x, y, z, core):
    return ((z % 2) * 4 + y) * 16 + (z // 2) * 8 + x * 2 + core


def send(value, move):
    pairs = [(d, index_of(*move(*place(d)))) for d in range(128)]
    return lax.ppermute(value, AXES, pairs)


def along_y(step):
    return lambda x, y, z, c: (x, (y + step) % RING, z, c)


def along_first(step):
    return lambda x, y, z, c: ((x + step) % RING, y, z, c) if c == 0 else (x, y, (z + step) % RING, c)


def along_second(step):
    return lambda x, y, z, c: (x, y, (z + step) % RING, c) if c == 0 else ((x + step) % RING, y, z, c)


def swap(x, y, z, c):
    return x, y, z, 1 - c


CHUNK = 256
BLOCK = 512
VMEM = pl.BlockSpec(memory_space=pltpu.VMEM)
SMEM = pl.BlockSpec(memory_space=pltpu.SMEM)
ANY = pl.BlockSpec(memory_space=pl.ANY)
HBM = pl.BlockSpec(memory_space=pltpu.HBM)


def prepare_kernel(text_ref, image_ref, text_bf, text_inv, image_bf, image_inv):
    for src, unit, inv in ((image_ref, image_bf, image_inv), (text_ref, text_bf, text_inv)):
        matrix = src[...]
        inverse = 1.0 / jnp.sqrt(jnp.sum(matrix * matrix, axis=1, keepdims=True) + 1e-06)
        inv[...] = inverse
        rows = (matrix * inverse).astype(jnp.bfloat16)
        if unit.ndim == 2:
            unit[...] = rows
        else:
            for i in range(unit.shape[0]):
                unit[i] = rows


def prepare(texts, images):
    return pl.pallas_call(
        prepare_kernel,
        out_shape=(
            jax.ShapeDtypeStruct((RING,) + texts.shape, jnp.bfloat16),
            jax.ShapeDtypeStruct((texts.shape[0], 1), jnp.float32),
            jax.ShapeDtypeStruct(images.shape, jnp.bfloat16),
            jax.ShapeDtypeStruct((images.shape[0], 1), jnp.float32),
        ),
        in_specs=[VMEM] * 2,
        out_specs=[VMEM] * 4,
    )(texts, images)


def nothing(*refs):
    pass


def held(value, others):
    return pl.pallas_call(
        nothing,
        out_shape=jax.ShapeDtypeStruct(value.shape, value.dtype),
        in_specs=[ANY] * (1 + len(others)),
        out_specs=ANY,
        input_output_aliases={0: 0},
    )(value, *others)


def after(value, others):
    for other in others:
        value = value + 0 * other[:1, : value.shape[1]].astype(value.dtype)
    return value


def finish_kernel(*refs):
    loss_parts, (image_out, text_out, loss_out) = refs[6], refs[7:]
    for (vectors, inverse, direction), out in ((refs[:3], image_out), (refs[3:6], text_out)):
        unit = vectors[...] * inverse[...]
        along = jnp.sum(unit * direction[...], axis=1, keepdims=True)
        out[...] = inverse[...] * (direction[...] - unit * along)
    total = jnp.sum(jnp.sum(loss_parts[...], axis=0), axis=1, keepdims=True)
    loss_out[...] = total * (1.0 / (128 * image_out.shape[0]))


def finish(images, texts, loss_parts):
    return pl.pallas_call(
        finish_kernel,
        out_shape=(
            jax.ShapeDtypeStruct(images[2].shape, jnp.float32),
            jax.ShapeDtypeStruct(texts[2].shape, jnp.float32),
            jax.ShapeDtypeStruct((1, 1), jnp.float32),
        ),
        in_specs=[VMEM] * 7,
        out_specs=[VMEM] * 3,
    )(*images, *texts, loss_parts)


def pair_kernel(n_image, *refs):
    scale_ref, base_ref, pick_ref, match_ref = refs[:4]
    halves, images, refs = refs[4:6], refs[6 : 6 + n_image], refs[6 + n_image :]
    text_outs, image_outs = refs[:2], refs[2 : 2 + n_image]
    loss_out, text_buf, image_buf, weight_buf, sems = refs[2 + n_image :]
    n_cols, n_text = n_image, 2 * RING

    def tile(i):
        return pl.ds(pl.multiple_of(i * CHUNK, CHUNK), CHUNK)

    image_copies = [
        pltpu.make_async_copy(piece, image_buf.at[tile(i)], sems.at[n_text + i])
        for i, piece in enumerate(images)
    ]
    text_copies = [
        pltpu.make_async_copy(
            halves[t // RING].at[tile(pick_ref[t % RING])], text_buf.at[tile(t)], sems.at[t]
        )
        for t in range(n_text)
    ]
    for copy in text_copies[:1] + image_copies + text_copies[1:]:
        copy.start()
    slope, shift, temperature = scale_ref[0], scale_ref[1], scale_ref[2]
    loss_out[...] = jnp.zeros_like(loss_out)
    row_index = lax.broadcasted_iota(jnp.int32, (CHUNK, CHUNK), 0)

    def weigh(t, carry):
        base = base_ref[t]
        pltpu.make_async_copy(text_buf.at[tile(t)], text_buf.at[tile(t)], sems.at[t]).wait()
        for i in range(n_cols):
            cols = pl.ds(i * CHUNK, CHUNK)
            scores = lax.dot_general(
                text_buf[tile(t), :],
                image_buf[cols, :],
                (((1,), (1,)), ((), ())),
                preferred_element_type=jnp.float32,
            )
            matched = (match_ref[:, cols] - base) == row_index
            power = scores * slope + shift
            grown = jnp.exp2(jnp.where(matched, -power, power))
            total = 1.0 + grown
            inv = pl.reciprocal(total, approx=True)
            inv = inv * (2.0 - total * inv)
            weight = (grown * temperature) * inv
            weight = jnp.where(matched, -weight, weight)
            weight_buf[tile(t), cols] = weight.astype(jnp.bfloat16)
            low, high = grown[: CHUNK // 2], grown[CHUNK // 2 :]
            joined = low + high + low * high
            low, high = joined[: CHUNK // 4], joined[CHUNK // 4 :]
            joined = low + high + low * high
            loss_out[...] += jnp.sum(jnp.log1p(joined).reshape(8, 8, CHUNK), axis=0)
        return carry

    for copy in image_copies:
        copy.wait()
    lax.fori_loop(0, n_text, weigh, 0)

    for half, out in enumerate(text_outs):
        rows = pl.ds(half * RING * CHUNK, RING * CHUNK)
        out[...] = jnp.dot(
            weight_buf[rows, :], image_buf[...], preferred_element_type=jnp.float32
        )

    for i, out in enumerate(image_outs):
        out[...] = lax.dot_general(
            weight_buf[:, pl.ds(i * CHUNK, CHUNK)],
            text_buf[...],
            (((0,), (0,)), ((), ())),
            preferred_element_type=jnp.float32,
        )


def slow(*arrays):
    return [pltpu.with_memory_space_constraint(a, pltpu.HBM) for a in arrays]


def pair_block(scale, base, pick, match, mine, other, images):
    n_image, dim = len(images), mine.shape[1]
    n_rows, n_cols = 2 * RING * CHUNK, n_image * CHUNK
    out_shape = [jax.ShapeDtypeStruct((n_rows // 2, dim), jnp.float32)] * 2
    out_shape += [jax.ShapeDtypeStruct((CHUNK, dim), jnp.float32)] * n_image
    out_shape += [jax.ShapeDtypeStruct((8, CHUNK), jnp.float32)]
    out = pl.pallas_call(
        functools.partial(pair_kernel, n_image),
        out_shape=out_shape,
        in_specs=[SMEM, SMEM, SMEM, VMEM, HBM, ANY] + [HBM] * n_image,
        out_specs=[VMEM] * len(out_shape),
        scratch_shapes=[
            pltpu.VMEM((n_rows, dim), jnp.bfloat16),
            pltpu.VMEM((n_cols, dim), jnp.bfloat16),
            pltpu.VMEM((n_rows, n_cols), jnp.bfloat16),
            pltpu.SemaphoreType.DMA((2 * RING + n_image,)),
        ],
        compiler_params=pltpu.CompilerParams(vmem_limit_bytes=VMEM_LIMIT),
        cost_estimate=pl.CostEstimate(
            flops=6 * n_rows * n_cols * dim,
            bytes_accessed=2 * (n_rows + n_cols) * dim,
            transcendentals=2 * n_rows * n_cols,
        ),
    )(scale, base, pick, match, *slow(mine), other, *slow(*images))
    return out[0], out[1], out[2:-1], out[-1]


VMEM_LIMIT = 32 * 2**20


def loss_parts(part):
    part = jnp.sum(part.reshape(-1, 128), axis=0)[None, None]
    parts = jnp.broadcast_to(part, (128, 1, 128))
    return lax.all_to_all(parts, AXES, 0, 0, tiled=True)


def narrow(part):
    return (part * 0.25).astype(WIRE)


def wide(part):
    return part.astype(jnp.float32) * 4.0


def body(
    picture_vectors, caption_vectors, matching_captions, natural_exponent_coefficient, learned_shift
):
    me = lax.axis_index("row") * 16 + lax.axis_index("col")
    x, y, z, core = place(me)
    image_rows, text_rows = picture_vectors.shape[0], caption_vectors.shape[0]
    temperature = jnp.exp(natural_exponent_coefficient[0])
    scale = jnp.stack([temperature * LOG2E, learned_shift[0] * LOG2E, temperature])

    own, text_inv, image_bf, image_inv = prepare(caption_vectors, picture_vectors)

    rings = {}
    for d in range(128):
        at = place(d)
        rings.setdefault(at[:1] + at[2:], []).append(d)
    mine = lax.all_to_all(own, AXES, 0, 0, axis_index_groups=list(rings.values()), tiled=True)
    mine = mine.reshape(RING * text_rows, -1)
    line = jnp.concatenate([image_bf] + [send(image_bf, along_first(-r)) for r in (1, 2, 3)])
    image_up, image_down = send(line, along_second(-1)), send(line, along_second(1))
    image_far = send(line, along_second(2))
    images = [line, image_up, image_down, image_far]
    mine = held(mine, images)
    other = send(mine, swap)

    pick = (jnp.arange(RING, dtype=jnp.int32) + y) % RING
    mine_base = index_of(x, pick, z, core) * text_rows
    other_base = index_of(x, pick, z, 1 - core) * text_rows
    table = matching_captions.reshape(-1, image_rows)
    first = jnp.arange(RING, dtype=jnp.int32)[None, :]
    second = jnp.array([0, 1, 3, 2], dtype=jnp.int32)[:, None]
    owners = jnp.where(
        core == 0,
        index_of((x + first) % RING, y, (z + second) % RING, core),
        index_of((x + second) % RING, y, (z + first) % RING, core),
    )
    match = jnp.take(table, owners.reshape(-1), axis=0).reshape(1, -1)

    n = text_rows
    base = jnp.concatenate([mine_base, other_base])
    mine, other, parts, loss = pair_block(scale, base, pick, match, mine, other, images)
    n = text_rows
    other = send(narrow(other), swap)
    wires = [
        lax.optimization_barrier(
            narrow(mine[s * n : (s + 1) * n] + wide(other[s * n : (s + 1) * n]))
        )
        for s in (1, 3, 2)
    ]
    text_dir = lax.optimization_barrier(mine[:n] + wide(other[:n]))
    for s, wire in zip((1, 3, 2), wires):
        text_dir = text_dir + wide(send(wire, along_y(s)))

    line_dir, up_part, down_part, far_part = parts
    far_part = after(far_part, [other])
    for s, part in ((1, up_part), (3, down_part), (2, far_part)):
        line_dir = line_dir + wide(send(narrow(part), along_second(s)))
    loss = loss_parts(after(loss, [line_dir]))
    n = image_rows
    wire = lax.optimization_barrier(narrow(line_dir[n:]))
    image_dir = line_dir[:n]
    for r in (1, 2, 3):
        image_dir = image_dir + wide(send(wire[(r - 1) * n : r * n], along_first(r)))

    image_dir, text_dir = [
        pltpu.with_memory_space_constraint(a, pltpu.VMEM) for a in (image_dir, text_dir)
    ]
    grad_images, grad_texts, loss = finish(
        (picture_vectors, image_inv, image_dir), (caption_vectors, text_inv, text_dir), loss
    )
    loss = loss[0, 0]
    return (grad_images, grad_texts, loss)


def solution(mesh):
    placed = (P(AXES, None), P(AXES, None), P(), P(), P())
    return jax.shard_map(
        body,
        mesh=mesh,
        in_specs=placed,
        out_specs=(P(AXES, None), P(AXES, None), P()),
        check_vma=False,
    )
```

```python
import functools
import math

import jax
import jax.numpy as jnp
from jax import lax
from jax.experimental import pallas as pl
from jax.experimental.pallas import tpu as pltpu
from jax.sharding import PartitionSpec as P

AXES = ("row", "col")
RING = 4
LOG2E = math.log2(math.e)
WIRE = jnp.float16


def place(index):
    row, col = index // 16, index % 16
    return (col // 2) % 4, row % 4, (col // 8) * 2 + row // 4, col % 2


def index_of(x, y, z, core):
    return ((z % 2) * 4 + y) * 16 + (z // 2) * 8 + x * 2 + core


def send(value, move):
    pairs = [(d, index_of(*move(*place(d)))) for d in range(128)]
    return lax.ppermute(value, AXES, pairs)


def along_y(step):
    return lambda x, y, z, c: (x, (y + step) % RING, z, c)


def along_first(step):
    return lambda x, y, z, c: ((x + step) % RING, y, z, c) if c == 0 else (x, y, (z + step) % RING, c)


def along_second(step):
    return lambda x, y, z, c: (x, y, (z + step) % RING, c) if c == 0 else ((x + step) % RING, y, z, c)


def swap(x, y, z, c):
    return x, y, z, 1 - c


CHUNK = 256
BLOCK = 512
VMEM = pl.BlockSpec(memory_space=pltpu.VMEM)
SMEM = pl.BlockSpec(memory_space=pltpu.SMEM)
ANY = pl.BlockSpec(memory_space=pl.ANY)
HBM = pl.BlockSpec(memory_space=pltpu.HBM)


def prepare_kernel(text_ref, image_ref, text_bf, text_inv, image_bf, image_inv):
    for src, unit, inv in ((image_ref, image_bf, image_inv), (text_ref, text_bf, text_inv)):
        matrix = src[...]
        inverse = 1.0 / jnp.sqrt(jnp.sum(matrix * matrix, axis=1, keepdims=True) + 1e-06)
        inv[...] = inverse
        rows = (matrix * inverse).astype(jnp.bfloat16)
        if unit.ndim == 2:
            unit[...] = rows
        else:
            for i in range(unit.shape[0]):
                unit[i] = rows


def prepare(texts, images):
    return pl.pallas_call(
        prepare_kernel,
        out_shape=(
            jax.ShapeDtypeStruct((RING,) + texts.shape, jnp.bfloat16),
            jax.ShapeDtypeStruct((texts.shape[0], 1), jnp.float32),
            jax.ShapeDtypeStruct(images.shape, jnp.bfloat16),
            jax.ShapeDtypeStruct((images.shape[0], 1), jnp.float32),
        ),
        in_specs=[VMEM] * 2,
        out_specs=[VMEM] * 4,
    )(texts, images)


def nothing(*refs):
    pass


def held(value, others):
    return pl.pallas_call(
        nothing,
        out_shape=jax.ShapeDtypeStruct(value.shape, value.dtype),
        in_specs=[ANY] * (1 + len(others)),
        out_specs=ANY,
        input_output_aliases={0: 0},
    )(value, *others)


def after(value, others):
    for other in others:
        value = value + 0 * other[:1, : value.shape[1]].astype(value.dtype)
    return value


def finish_kernel(*refs):
    loss_parts, (image_out, text_out, loss_out) = refs[6], refs[7:]
    for (vectors, inverse, direction), out in ((refs[:3], image_out), (refs[3:6], text_out)):
        unit = vectors[...] * inverse[...]
        along = jnp.sum(unit * direction[...], axis=1, keepdims=True)
        out[...] = inverse[...] * (direction[...] - unit * along)
    total = jnp.sum(jnp.sum(loss_parts[...], axis=0), axis=1, keepdims=True)
    loss_out[...] = total * (1.0 / (128 * image_out.shape[0]))


def finish(images, texts, loss_parts):
    return pl.pallas_call(
        finish_kernel,
        out_shape=(
            jax.ShapeDtypeStruct(images[2].shape, jnp.float32),
            jax.ShapeDtypeStruct(texts[2].shape, jnp.float32),
            jax.ShapeDtypeStruct((1, 1), jnp.float32),
        ),
        in_specs=[VMEM] * 7,
        out_specs=[VMEM] * 3,
    )(*images, *texts, loss_parts)


def pair_kernel(n_image, *refs):
    scale_ref, base_ref, pick_ref, match_ref = refs[:4]
    halves, images, refs = refs[4:6], refs[6 : 6 + n_image], refs[6 + n_image :]
    text_outs, image_outs = refs[:2], refs[2 : 2 + n_image]
    loss_out, text_buf, image_buf, weight_buf, sems = refs[2 + n_image :]
    n_cols, n_text = n_image, 2 * RING

    def tile(i):
        return pl.ds(pl.multiple_of(i * CHUNK, CHUNK), CHUNK)

    image_copies = [
        pltpu.make_async_copy(piece, image_buf.at[tile(i)], sems.at[n_text + i])
        for i, piece in enumerate(images)
    ]
    text_copies = [
        pltpu.make_async_copy(
            halves[t // RING].at[tile(pick_ref[t % RING])], text_buf.at[tile(t)], sems.at[t]
        )
        for t in range(n_text)
    ]
    for copy in text_copies[:1] + image_copies + text_copies[1:]:
        copy.start()
    slope, shift, temperature = scale_ref[0], scale_ref[1], scale_ref[2]
    loss_out[...] = jnp.zeros_like(loss_out)
    row_index = lax.broadcasted_iota(jnp.int32, (CHUNK, CHUNK), 0)

    def weigh(t, carry):
        base = base_ref[t]
        pltpu.make_async_copy(text_buf.at[tile(t)], text_buf.at[tile(t)], sems.at[t]).wait()
        for i in range(n_cols):
            cols = pl.ds(i * CHUNK, CHUNK)
            scores = lax.dot_general(
                text_buf[tile(t), :],
                image_buf[cols, :],
                (((1,), (1,)), ((), ())),
                preferred_element_type=jnp.float32,
            )
            matched = (match_ref[:, cols] - base) == row_index
            power = scores * slope + shift
            grown = jnp.exp2(jnp.where(matched, -power, power))
            total = 1.0 + grown
            inv = pl.reciprocal(total, approx=True)
            inv = inv * (2.0 - total * inv)
            weight = (grown * temperature) * inv
            weight = jnp.where(matched, -weight, weight)
            weight_buf[tile(t), cols] = weight.astype(jnp.bfloat16)
            low, high = grown[: CHUNK // 2], grown[CHUNK // 2 :]
            joined = low + high + low * high
            low, high = joined[: CHUNK // 4], joined[CHUNK // 4 :]
            joined = low + high + low * high
            loss_out[...] += jnp.sum(jnp.log1p(joined).reshape(8, 8, CHUNK), axis=0)
        return carry

    for copy in image_copies:
        copy.wait()
    lax.fori_loop(0, n_text, weigh, 0)

    for half, out in enumerate(text_outs):
        rows = pl.ds(half * RING * CHUNK, RING * CHUNK)
        out[...] = jnp.dot(
            weight_buf[rows, :], image_buf[...], preferred_element_type=jnp.float32
        )

    for i, out in enumerate(image_outs):
        out[...] = lax.dot_general(
            weight_buf[:, pl.ds(i * CHUNK, CHUNK)],
            text_buf[...],
            (((0,), (0,)), ((), ())),
            preferred_element_type=jnp.float32,
        )


def slow(*arrays):
    return [pltpu.with_memory_space_constraint(a, pltpu.HBM) for a in arrays]


def pair_block(scale, base, pick, match, mine, other, images):
    n_image, dim = len(images), mine.shape[1]
    n_rows, n_cols = 2 * RING * CHUNK, n_image * CHUNK
    out_shape = [jax.ShapeDtypeStruct((n_rows // 2, dim), jnp.float32)] * 2
    out_shape += [jax.ShapeDtypeStruct((CHUNK, dim), jnp.float32)] * n_image
    out_shape += [jax.ShapeDtypeStruct((8, CHUNK), jnp.float32)]
    out = pl.pallas_call(
        functools.partial(pair_kernel, n_image),
        out_shape=out_shape,
        in_specs=[SMEM, SMEM, SMEM, VMEM, HBM, ANY] + [HBM] * n_image,
        out_specs=[VMEM] * len(out_shape),
        scratch_shapes=[
            pltpu.VMEM((n_rows, dim), jnp.bfloat16),
            pltpu.VMEM((n_cols, dim), jnp.bfloat16),
            pltpu.VMEM((n_rows, n_cols), jnp.bfloat16),
            pltpu.SemaphoreType.DMA((2 * RING + n_image,)),
        ],
        compiler_params=pltpu.CompilerParams(vmem_limit_bytes=VMEM_LIMIT),
        cost_estimate=pl.CostEstimate(
            flops=6 * n_rows * n_cols * dim,
            bytes_accessed=2 * (n_rows + n_cols) * dim,
            transcendentals=2 * n_rows * n_cols,
        ),
    )(scale, base, pick, match, *slow(mine), other, *slow(*images))
    return out[0], out[1], out[2:-1], out[-1]


VMEM_LIMIT = 32 * 2**20


def loss_parts(part):
    part = jnp.sum(part.reshape(-1, 128), axis=0)[None, None]
    parts = jnp.broadcast_to(part, (128, 1, 128))
    return lax.all_to_all(parts, AXES, 0, 0, tiled=True)


def narrow(part):
    return (part * 0.25).astype(WIRE)


def wide(part):
    return part.astype(jnp.float32) * 4.0


def body(
    picture_vectors, caption_vectors, matching_captions, natural_exponent_coefficient, learned_shift
):
    me = lax.axis_index("row") * 16 + lax.axis_index("col")
    x, y, z, core = place(me)
    image_rows, text_rows = picture_vectors.shape[0], caption_vectors.shape[0]
    temperature = jnp.exp(natural_exponent_coefficient[0])
    scale = jnp.stack([temperature * LOG2E, learned_shift[0] * LOG2E, temperature])

    own, text_inv, image_bf, image_inv = prepare(caption_vectors, picture_vectors)

    rings = {}
    for d in range(128):
        at = place(d)
        rings.setdefault(at[:1] + at[2:], []).append(d)
    mine = lax.all_to_all(own, AXES, 0, 0, axis_index_groups=list(rings.values()), tiled=True)
    mine = mine.reshape(RING * text_rows, -1)
    line = jnp.concatenate([image_bf] + [send(image_bf, along_first(-r)) for r in (1, 2, 3)])
    image_up, image_down = send(line, along_second(-1)), send(line, along_second(1))
    image_far = send(line, along_second(2))
    images = [line, image_up, image_down, image_far]
    mine = held(mine, images)
    other = send(mine, swap)

    pick = (jnp.arange(RING, dtype=jnp.int32) + y) % RING
    mine_base = index_of(x, pick, z, core) * text_rows
    other_base = index_of(x, pick, z, 1 - core) * text_rows
    table = matching_captions.reshape(-1, image_rows)
    first = jnp.arange(RING, dtype=jnp.int32)[None, :]
    second = jnp.array([0, 1, 3, 2], dtype=jnp.int32)[:, None]
    owners = jnp.where(
        core == 0,
        index_of((x + first) % RING, y, (z + second) % RING, core),
        index_of((x + second) % RING, y, (z + first) % RING, core),
    )
    match = jnp.take(table, owners.reshape(-1), axis=0).reshape(1, -1)

    n = text_rows
    base = jnp.concatenate([mine_base, other_base])
    mine, other, parts, loss = pair_block(scale, base, pick, match, mine, other, images)
    n = text_rows
    other = send(narrow(other), swap)
    wires = [
        lax.optimization_barrier(
            narrow(mine[s * n : (s + 1) * n] + wide(other[s * n : (s + 1) * n]))
        )
        for s in (1, 3, 2)
    ]
    text_dir = lax.optimization_barrier(mine[:n] + wide(other[:n]))
    for s, wire in zip((1, 3, 2), wires):
        text_dir = text_dir + wide(send(wire, along_y(s)))

    line_dir, up_part, down_part, far_part = parts
    down_part, far_part = after(down_part, [other]), after(far_part, [other])
    for s, part in ((1, up_part), (3, down_part), (2, far_part)):
        line_dir = line_dir + wide(send(narrow(part), along_second(s)))
    loss = loss_parts(after(loss, [line_dir]))
    n = image_rows
    wire = lax.optimization_barrier(narrow(line_dir[n:]))
    image_dir = line_dir[:n]
    for r in (1, 2, 3):
        image_dir = image_dir + wide(send(wire[(r - 1) * n : r * n], along_first(r)))

    image_dir, text_dir = [
        pltpu.with_memory_space_constraint(a, pltpu.VMEM) for a in (image_dir, text_dir)
    ]
    grad_images, grad_texts, loss = finish(
        (picture_vectors, image_inv, image_dir), (caption_vectors, text_inv, text_dir), loss
    )
    loss = loss[0, 0]
    return (grad_images, grad_texts, loss)


def solution(mesh):
    placed = (P(AXES, None), P(AXES, None), P(), P(), P())
    return jax.shard_map(
        body,
        mesh=mesh,
        in_specs=placed,
        out_specs=(P(AXES, None), P(AXES, None), P()),
        check_vma=False,
    )
```
